32 devices in a mesh: paths: 2 (over x), node: 16 (over z, y, core).
Axes of the slice: x: 2, y: 2, z: 4, core: 2. Of those that a mesh axis runs over, the one named last changes fastest.
Arguments:
- amplitudes: float32 [2, 2097152], P(None, ('paths', 'node')), parts along dimension 1, may hold values from -6 to 6
- gates: float32 [2, 12, 128, 128], replicated, may hold values from -0.375 to 0.375
Outputs:
- final_state: float32 [2, 2097152], P(None, ('paths', 'node')), parts along dimension 1
The draws below stay inside these ranges and needn't reach their ends.
There are 2 independent parts, one for each index of `paths`. The reference program is written for one: setup_inputs(seed, part) draws one part's arguments, and reference() takes and returns one part's arrays. A program takes and returns all parts, laid end to end along the dimension named above; an argument that names none is the same for every part. Nothing has to cross between parts.
All inputs are finite; a program needn't handle non-finite values.
Results may differ from the reference program's by a relative error of at most 0.0001.
Values sent between devices are 32-bit elements; how exact they have to be, the bound alone decides.
A program may use at most 64 MiB of HBM per device.

```python
import jax
import jax.numpy as jnp
from jax import lax

LOC = 65536
GORDER = 128
GATES = 12
AMPS = 1048576
N_NODE = 16


def shard_levels(stream_key, extent, pieces, smallest, largest):
    gain, own = 1.0, jax.random.fold_in(stream_key, 6)
    for axis_at, shards_of in pieces:
        heights = jnp.exp(jax.random.uniform(jax.random.fold_in(own, axis_at), (shards_of,), jnp.float32, smallest / len(pieces), largest / len(pieces)))
        gain = gain * jnp.repeat(heights, extent[axis_at] // shards_of).reshape([-1 if axis == axis_at else 1 for axis in range(len(extent))])
    return gain


def normal_values(key, dims, scale, reach, pieces=(), dtype=jnp.bfloat16):
    array = scale * jax.random.normal(key, dims, jnp.float32)
    if pieces:
        array = array * shard_levels(key, dims, pieces, -0.22, 0.18)
    return jnp.clip(array, -reach, reach).astype(dtype)


def setup_inputs(seed: int = 0, part: int = 0) -> dict:
    keys = jax.random.split(jax.random.key(seed), 3)
    part_keys = jax.random.split(jax.random.fold_in(keys[2], part), 3)
    amplitudes = normal_values(part_keys[0], (2, AMPS), 1.0, 6.0, ((1, 16),), jnp.float32)
    gates = normal_values(keys[1], (2, GATES, GORDER, GORDER), (2 * GORDER) ** -0.5, 0.375, (), jnp.float32)
    return {"amplitudes": amplitudes, "gates": gates}


def apply_gate(state, gate_pair, offset):
    total = state.shape[1]
    inner = 1 << offset
    view = state.reshape(2, total // (128 * inner), 128, inner)
    real_in, imag_in = view[0], view[1]
    real_g, imag_g = gate_pair[0], gate_pair[1]
    hp = lax.Precision.HIGHEST
    real_out = jnp.einsum('ij,ajb->aib', real_g, real_in, precision=hp) - jnp.einsum('ij,ajb->aib', imag_g, imag_in, precision=hp)
    imag_out = jnp.einsum('ij,ajb->aib', real_g, imag_in, precision=hp) + jnp.einsum('ij,ajb->aib', imag_g, real_in, precision=hp)
    return jnp.stack([real_out, imag_out], 0).reshape(2, total)


def swap_bits(state, low, high):
    total = state.shape[1]
    view = state.reshape(2, total >> (high + 1), 2, (1 << high) >> (low + 1), 2, 1 << low)
    view = jnp.swapaxes(view, 2, 4)
    return view.reshape(2, total)


def run_section(state, gates, first, offsets):
    distinct = gates.shape[1]
    for step in range(4):
        state = apply_gate(state, gates[:, (first + step) % distinct], offsets[step])
    return state


def reference(amplitudes, gates):
    locq = int(LOC).bit_length() - 1
    globq = int(N_NODE).bit_length() - 1
    offsets = [0, (locq - 7) // 2, locq - 7, locq - 9]
    state = run_section(amplitudes, gates, 0, offsets)
    for k in range(3):
        state = swap_bits(state, locq - 1 - k, locq + k)
    state = run_section(state, gates, 4, offsets)
    count = 1 << globq
    total = state.shape[1]
    view = state.reshape(2, count, count, total // (count * count))
    state = jnp.swapaxes(view, 1, 2).reshape(2, total)
    return run_section(state, gates, 8, offsets)
```

```python
import functools

import jax
import jax.numpy as jnp
from jax import lax
from jax.experimental import pallas as pl
from jax.experimental.pallas import tpu as pltpu
from jax.sharding import PartitionSpec as P

F32 = jnp.float32
BF16 = jnp.bfloat16
ORDER = 128
LANES = 128
QUARTERS = 4


def split(x):
    high = x.astype(BF16)
    low = (x - high.astype(F32)).astype(BF16)
    return high, low


def exchange_bits(groups):
    lane = lax.broadcasted_iota(jnp.int32, groups[0].shape, 1)
    turned = [groups[0]] + [pltpu.roll(groups[i], 16 * i, 1) for i in range(1, 8)]
    turned = [turned[-i % 8] for i in range(8)]
    for k in range(3):
        here = (lane & (16 << k)) == 0
        turned = [jnp.where(here, turned[i], turned[(i - (1 << k)) % 8]) for i in range(8)]
    return [turned[0]] + [pltpu.roll(turned[i], LANES - 16 * i, 1) for i in range(1, 8)]


def swap_blocks(y):
    columns = []
    for start in range(0, y.shape[1], LANES):
        parts = []
        for base in range(0, 2 * ORDER, ORDER):
            parts += exchange_bits(
                [y[base + 16 * i : base + 16 * i + 16, start : start + LANES] for i in range(8)]
            )
        columns.append(jnp.concatenate(parts, 0))
    return jnp.concatenate(columns, 1)


def to_left(y):
    return jnp.concatenate(
        [
            jnp.concatenate([y[i : i + ORDER, :LANES], y[i : i + ORDER, LANES:]], 0)
            for i in range(0, y.shape[0], ORDER)
        ],
        1,
    )


def to_right(y):
    return jnp.concatenate(
        [
            jnp.concatenate([y[:ORDER, i : i + LANES], y[ORDER:, i : i + LANES]], 1)
            for i in range(0, y.shape[1], LANES)
        ],
        0,
    )


def prepare(g_ref, gc_ref, m, permuted):
    real_high, real_low = split(g_ref[0, m])
    imag_high, imag_low = split(g_ref[1, m])
    blocks = [real_high, real_low, imag_high, imag_low]
    if permuted:
        row = lax.broadcasted_iota(jnp.int32, (ORDER, ORDER), 0)
        column = lax.broadcasted_iota(jnp.int32, (ORDER, ORDER), 1)
        place = ((row & 15) << 3) + (row >> 4)
        move = jnp.where(column == place, 1.0, 0.0).astype(BF16)
        wide = jnp.dot(move, jnp.concatenate(blocks, 1), preferred_element_type=F32).astype(BF16)
        blocks = [
            lax.dot_general(
                wide[:, i * ORDER : (i + 1) * ORDER], move, (((1,), (1,)), ((), ())), preferred_element_type=F32
            ).astype(BF16)
            for i in range(4)
        ]
    real_high, real_low, imag_high, imag_low = blocks
    gc_ref[m, :ORDER, :] = jnp.concatenate([real_high, -imag_high, real_low, -imag_low, real_high, -imag_high], 1)
    gc_ref[m, ORDER:, :] = jnp.concatenate([imag_high, real_high, imag_low, real_low, imag_high, real_high], 1)


def prepare_halves(g_ref, gh_ref, k, m):
    real, imag = g_ref[0, m], g_ref[1, m]
    half = ORDER // 2
    below = lax.broadcasted_iota(jnp.int32, (ORDER, ORDER), 1) < half

    def fold(a, b):
        return jnp.where(below, a, pltpu.roll(b, half, 1)), jnp.where(below, pltpu.roll(a, half, 1), b)

    for part, sides in enumerate((fold(real, -imag), fold(imag, real))):
        for h in range(2):
            high, low = split(sides[h])
            gh_ref[k, h, part * ORDER : (part + 1) * ORDER, :] = jnp.concatenate([high, low, high], 1)


def left(gate, x):
    high, low = split(x)
    return jnp.dot(gate, jnp.concatenate([high, high, low], 0), preferred_element_type=F32)


def right(gate, x):
    high, low = split(x)
    return lax.dot_general(
        jnp.concatenate([high, high, low], 1), gate, (((1,), (1,)), ((), ())), preferred_element_type=F32
    )


def reversed3(x):
    return ((x & 1) << 2) | (x & 2) | ((x >> 2) & 1)


def kernel(
    nodes, distinct, x_hbm, g_hbm, o_ref, x_ref, g_ref, gc, gh, sa, sb, sc, sd, r1, r2, in_x, in_g, send1, recv1, send2, recv2
):
    rows = sa.shape[1]
    quarter = rows // QUARTERS

    def load_x(a):
        some = pl.ds(2 * a * quarter, 2 * quarter)
        return pltpu.make_async_copy(x_hbm.at[some, :], x_ref.at[some, :], in_x.at[a])

    def load_gate(m):
        return pltpu.make_async_copy(g_hbm.at[:, m], g_ref.at[:, m], in_g.at[m])

    sequence = list(dict.fromkeys(g % distinct for g in (0, 1, 2, 3, 4, 5, 8, 6, 7, 9, 10, 11)))
    for m in sequence[:2]:
        load_gate(m).start()
    for a in range(QUARTERS):
        load_x(a).start()
    for m in sequence[2:]:
        load_gate(m).start()
    me = lax.axis_index("node")
    barrier = pltpu.get_barrier_semaphore()
    for i in range(1, nodes):
        pl.semaphore_signal(barrier, inc=1, device_id={"node": me ^ i}, device_id_type=pl.DeviceIdType.MESH)

    ready = set()
    loaded = set()

    def arrive(m):
        if m not in loaded:
            loaded.add(m)
            load_gate(m).wait()

    def gate(g):
        m = g % distinct
        if m not in ready:
            ready.add(m)
            arrive(m)
            prepare(g_ref, gc, m, g % 4 == 1)
        return gc[m]

    def store(ref, first, y):
        ref[0, pl.ds(first, y.shape[0]), :] = y[:, :LANES]
        ref[1, pl.ds(first, y.shape[0]), :] = y[:, LANES:]

    def load_quarters(ref, firsts):
        return jnp.concatenate(
            [
                jnp.concatenate([ref[0, pl.ds(first, quarter), :], ref[1, pl.ds(first, quarter), :]], 0)
                for first in firsts
            ],
            1,
        )

    def store_quarters(ref, firsts, y):
        for i, first in enumerate(firsts):
            ref[0, pl.ds(first, quarter), :] = y[:ORDER, i * LANES : (i + 1) * LANES]
            ref[1, pl.ds(first, quarter), :] = y[ORDER:, i * LANES : (i + 1) * LANES]

    def strided(g, src, dst):
        matrix = gate(g)
        for pair in range(2):
            x = jnp.concatenate(
                [
                    jnp.concatenate([src[part, pl.ds(2 * pair + c, ORDER, stride=4), :] for part in range(2)], 0)
                    for c in range(2)
                ],
                1,
            )
            y = left(matrix, x)
            for c in range(2):
                for part in range(2):
                    dst[part, pl.ds(2 * pair + c, ORDER, stride=4), :] = y[
                        part * ORDER : (part + 1) * ORDER, c * LANES : (c + 1) * LANES
                    ]

    def halves_of(g, k):
        arrive(g % distinct)
        prepare_halves(g_ref, gh, k, g % distinct)

    def strided_half(k, src, dst, h, add):
        matrix = gh[k, h]
        base = pl.multiple_of(h * (rows // 2), rows // 2)
        for pair in range(2):
            x = jnp.concatenate(
                [
                    jnp.concatenate(
                        [src[part, pl.ds(base + 2 * pair + c, ORDER // 2, stride=4), :] for part in range(2)], 0
                    )
                    for c in range(2)
                ],
                1,
            )
            y = left(matrix, x)
            for c in range(2):
                for part in range(2):
                    z = y[part * ORDER : (part + 1) * ORDER, c * LANES : (c + 1) * LANES]
                    some = pl.ds(2 * pair + c, ORDER, stride=4)
                    if add:
                        z = z + dst[part, some, :]
                    dst[part, some, :] = z

    def middle(g, y):
        return swap_blocks(left(gate(g), swap_blocks(y)))

    def low_gates(x):
        y = to_right(middle(5, to_left(right(gate(4), x))))
        return right(gate(8), y)

    halves = [(0, quarter, 2 * quarter, 3 * quarter)]
    gate(0)
    gate(1)
    for a in range(QUARTERS):
        load_x(a).wait()
    x = jnp.concatenate([x_ref[pl.ds(part, rows, stride=2), :] for part in range(2)], 1)
    store(sa, 0, to_right(middle(1, to_left(right(gate(0), x)))))
    gate(2)
    gate(3)
    strided(2, sa, sb)
    pl.semaphore_wait(barrier, nodes - 1)

    slot = reversed3(me & 7)
    part1 = rows // 8
    copies = []
    for orders in ((1, 0), (3, 2)):
        spots = [(slot >> 1) ^ order for order in orders]
        firsts = [pl.multiple_of(a * quarter, quarter) for a in spots]
        y = left(gate(3), load_quarters(sb, firsts))
        if 0 in orders:
            store_quarters(sc, firsts, y)
        else:
            y = low_gates(to_right(y))
            for i, first in enumerate(firsts):
                store(sc, first, y[i * quarter : (i + 1) * quarter])
        for order, a, low in [(order, a, low) for order, a in zip(orders, spots) for low in (1, 0)]:
            if order == 0 and low == 0:
                mine = pl.ds(pl.multiple_of(slot * part1, part1), part1)
                r1[:, mine, :] = sc[:, mine, :]
                continue
            block = 2 * a + ((slot & 1) ^ low)
            index = 2 * order + low
            copy = pltpu.make_async_remote_copy(
                src_ref=sc.at[:, pl.ds(pl.multiple_of(block * part1, part1), part1), :],
                dst_ref=r1.at[:, pl.ds(pl.multiple_of(slot * part1, part1), part1), :],
                send_sem=send1.at[index],
                recv_sem=recv1.at[index],
                device_id={"node": (me & ~7) | reversed3(block)},
                device_id_type=pl.DeviceIdType.MESH,
            )
            copy.start()
            copies.append((index, copy))

    halves_of(6, 0)
    gate(7)
    gate(9)

    arrivals = dict(copies)
    firsts = []
    for index in range(4):
        if index in arrivals:
            arrivals[index].wait_recv()
        firsts.append(pl.multiple_of((slot ^ index) * part1, part1))
    x = jnp.concatenate(
        [jnp.concatenate([r1[part, pl.ds(first, part1), :] for part in range(2)], 1) for first in firsts], 0
    )
    y = low_gates(x)
    for i, first in enumerate(firsts):
        store(sa, first, y[i * part1 : (i + 1) * part1])
    strided_half(0, sa, sb, slot >> 2, False)
    for index in range(4, 8):
        arrivals[index].wait_recv()
    strided_half(0, r1, sb, (slot >> 2) ^ 1, True)

    part2 = rows // nodes
    per = nodes // QUARTERS
    early = part2 * LANES >= 1 << 11
    second = []
    mine = pl.ds(pl.multiple_of(me * part2, part2), part2)
    for orders in ((2,), (3,), (1, 0)):
        firsts = [pl.multiple_of(((me // per) ^ order) * quarter, quarter) for order in orders]
        y = left(gate(7), load_quarters(sb, firsts))
        if early:
            y = middle(9, y)
        store_quarters(sd, firsts, y)
        for order, low in [(order, low) for order in orders for low in range(per - 1, -1, -1)]:
            if order == 0 and low == 0:
                r2[:, mine, :] = sd[:, mine, :]
                continue
            block = me ^ (order * per + low)
            index = order * per + low
            copy = pltpu.make_async_remote_copy(
                src_ref=sd.at[:, pl.ds(pl.multiple_of(block * part2, part2), part2), :],
                dst_ref=r2.at[:, mine, :],
                send_sem=send2.at[index],
                recv_sem=recv2.at[index],
                device_id={"node": block},
                device_id_type=pl.DeviceIdType.MESH,
            )
            copy.start()
            second.append((index, copy))

    halves_of(10, 1)
    gate(11)
    for _, copy in copies:
        copy.wait_send()
    side = me // (nodes // 2)
    if early:
        for far in range(2):
            for index, copy in second:
                if index // (nodes // 2) == far:
                    copy.wait_recv()
            strided_half(1, r2, sa, side ^ far, far == 1)
    else:
        for _, copy in second:
            copy.wait_recv()
        for firsts in halves:
            store_quarters(sb, firsts, middle(9, load_quarters(r2, firsts)))
        for far in range(2):
            strided_half(1, sb, sa, side ^ far, far == 1)
    for firsts in halves:
        y = left(gate(11), load_quarters(sa, firsts))
        for i, first in enumerate(firsts):
            for part in range(2):
                o_ref[pl.ds(2 * first + part, quarter, stride=2), :] = y[
                    part * ORDER : (part + 1) * ORDER, i * LANES : (i + 1) * LANES
                ]
    for _, copy in second:
        copy.wait_send()


def body(nodes, amplitudes, gates):
    total = amplitudes.shape[1]
    distinct = gates.shape[1]
    rows = total // LANES
    x = amplitudes.reshape(2, rows, LANES).transpose(1, 0, 2).reshape(2 * rows, LANES)
    state = pltpu.VMEM((2, rows, LANES), F32)
    out = pl.pallas_call(
        functools.partial(kernel, nodes, distinct),
        out_shape=jax.ShapeDtypeStruct((2 * rows, LANES), F32),
        in_specs=[pl.BlockSpec(memory_space=pltpu.HBM)] * 2,
        out_specs=pl.BlockSpec(memory_space=pltpu.VMEM),
        scratch_shapes=[
            pltpu.VMEM((2 * rows, LANES), F32),
            pltpu.VMEM(gates.shape, F32),
            pltpu.VMEM((distinct, 2 * ORDER, 6 * ORDER), BF16),
            pltpu.VMEM((2, 2, 2 * ORDER, 3 * ORDER), BF16),
            state,
            state,
            state,
            state,
            state,
            state,
            pltpu.SemaphoreType.DMA((QUARTERS,)),
            pltpu.SemaphoreType.DMA((distinct,)),
            pltpu.SemaphoreType.DMA((8,)),
            pltpu.SemaphoreType.DMA((8,)),
            pltpu.SemaphoreType.DMA((nodes,)),
            pltpu.SemaphoreType.DMA((nodes,)),
        ],
        compiler_params=pltpu.CompilerParams(collective_id=0, has_side_effects=True, vmem_limit_bytes=53 << 20),
        name="circuit",
    )(x, gates)
    return out.reshape(rows, 2, LANES).transpose(1, 0, 2).reshape(2, total)


def solution(mesh):
    spec = P(None, ("paths", "node"))
    return jax.shard_map(
        functools.partial(body, mesh.shape["node"]), mesh=mesh, in_specs=(spec, P()), out_specs=spec, check_vma=False
    )
```

```python
import functools

import jax
import jax.numpy as jnp
from jax import lax
from jax.experimental import pallas as pl
from jax.experimental.pallas import tpu as pltpu
from jax.sharding import PartitionSpec as P

F32 = jnp.float32
BF16 = jnp.bfloat16
ORDER = 128
LANES = 128
QUARTERS = 4


def split(x):
    high = x.astype(BF16)
    low = (x - high.astype(F32)).astype(BF16)
    return high, low


def exchange_bits(groups):
    lane = lax.broadcasted_iota(jnp.int32, groups[0].shape, 1)
    turned = [groups[0]] + [pltpu.roll(groups[i], 16 * i, 1) for i in range(1, 8)]
    turned = [turned[-i % 8] for i in range(8)]
    for k in range(3):
        here = (lane & (16 << k)) == 0
        turned = [jnp.where(here, turned[i], turned[(i - (1 << k)) % 8]) for i in range(8)]
    return [turned[0]] + [pltpu.roll(turned[i], LANES - 16 * i, 1) for i in range(1, 8)]


def swap_blocks(y):
    columns = []
    for start in range(0, y.shape[1], LANES):
        parts = []
        for base in range(0, 2 * ORDER, ORDER):
            parts += exchange_bits(
                [y[base + 16 * i : base + 16 * i + 16, start : start + LANES] for i in range(8)]
            )
        columns.append(jnp.concatenate(parts, 0))
    return jnp.concatenate(columns, 1)


def to_left(y):
    return jnp.concatenate(
        [
            jnp.concatenate([y[i : i + ORDER, :LANES], y[i : i + ORDER, LANES:]], 0)
            for i in range(0, y.shape[0], ORDER)
        ],
        1,
    )


def to_right(y):
    return jnp.concatenate(
        [
            jnp.concatenate([y[:ORDER, i : i + LANES], y[ORDER:, i : i + LANES]], 1)
            for i in range(0, y.shape[1], LANES)
        ],
        0,
    )


def prepare(g_ref, gc_ref, m, permuted):
    real_high, real_low = split(g_ref[0, m])
    imag_high, imag_low = split(g_ref[1, m])
    blocks = [real_high, real_low, imag_high, imag_low]
    if permuted:
        row = lax.broadcasted_iota(jnp.int32, (ORDER, ORDER), 0)
        column = lax.broadcasted_iota(jnp.int32, (ORDER, ORDER), 1)
        place = ((row & 15) << 3) + (row >> 4)
        move = jnp.where(column == place, 1.0, 0.0).astype(BF16)
        wide = jnp.dot(move, jnp.concatenate(blocks, 1), preferred_element_type=F32).astype(BF16)
        blocks = [
            lax.dot_general(
                wide[:, i * ORDER : (i + 1) * ORDER], move, (((1,), (1,)), ((), ())), preferred_element_type=F32
            ).astype(BF16)
            for i in range(4)
        ]
    real_high, real_low, imag_high, imag_low = blocks
    gc_ref[m, :ORDER, :] = jnp.concatenate([real_high, -imag_high, real_low, -imag_low, real_high, -imag_high], 1)
    gc_ref[m, ORDER:, :] = jnp.concatenate([imag_high, real_high, imag_low, real_low, imag_high, real_high], 1)


def prepare_halves(g_ref, gh_ref, k, m):
    real, imag = g_ref[0, m], g_ref[1, m]
    half = ORDER // 2
    below = lax.broadcasted_iota(jnp.int32, (ORDER, ORDER), 1) < half

    def fold(a, b):
        return jnp.where(below, a, pltpu.roll(b, half, 1)), jnp.where(below, pltpu.roll(a, half, 1), b)

    for part, sides in enumerate((fold(real, -imag), fold(imag, real))):
        for h in range(2):
            high, low = split(sides[h])
            gh_ref[k, h, part * ORDER : (part + 1) * ORDER, :] = jnp.concatenate([high, low, high], 1)


def left(gate, x):
    high, low = split(x)
    return jnp.dot(gate, jnp.concatenate([high, high, low], 0), preferred_element_type=F32)


def right(gate, x):
    high, low = split(x)
    return lax.dot_general(
        jnp.concatenate([high, high, low], 1), gate, (((1,), (1,)), ((), ())), preferred_element_type=F32
    )


def reversed3(x):
    return ((x & 1) << 2) | (x & 2) | ((x >> 2) & 1)


def kernel(
    nodes, distinct, x_hbm, g_hbm, o_ref, x_ref, g_ref, gc, gh, sa, sb, sc, sd, r1, r2, in_x, in_g, send1, recv1, send2, recv2
):
    rows = sa.shape[1]
    quarter = rows // QUARTERS

    def load_x(a):
        some = pl.ds(2 * a * quarter, 2 * quarter)
        return pltpu.make_async_copy(x_hbm.at[some, :], x_ref.at[some, :], in_x.at[a])

    def load_gate(m):
        return pltpu.make_async_copy(g_hbm.at[:, m], g_ref.at[:, m], in_g.at[m])

    sequence = list(dict.fromkeys(g % distinct for g in (0, 1, 2, 3, 4, 5, 8, 6, 7, 9, 10, 11)))
    for m in sequence[:2]:
        load_gate(m).start()
    for a in range(QUARTERS):
        load_x(a).start()
    for m in sequence[2:]:
        load_gate(m).start()
    me = lax.axis_index("node")
    barrier = pltpu.get_barrier_semaphore()
    for i in range(1, nodes):
        pl.semaphore_signal(barrier, inc=1, device_id={"node": me ^ i}, device_id_type=pl.DeviceIdType.MESH)

    ready = set()
    loaded = set()

    def arrive(m):
        if m not in loaded:
            loaded.add(m)
            load_gate(m).wait()

    def gate(g):
        m = g % distinct
        if m not in ready:
            ready.add(m)
            arrive(m)
            prepare(g_ref, gc, m, g % 4 == 1)
        return gc[m]

    def store(ref, first, y):
        ref[0, pl.ds(first, y.shape[0]), :] = y[:, :LANES]
        ref[1, pl.ds(first, y.shape[0]), :] = y[:, LANES:]

    def load_quarters(ref, firsts):
        return jnp.concatenate(
            [
                jnp.concatenate([ref[0, pl.ds(first, quarter), :], ref[1, pl.ds(first, quarter), :]], 0)
                for first in firsts
            ],
            1,
        )

    def store_quarters(ref, firsts, y):
        for i, first in enumerate(firsts):
            ref[0, pl.ds(first, quarter), :] = y[:ORDER, i * LANES : (i + 1) * LANES]
            ref[1, pl.ds(first, quarter), :] = y[ORDER:, i * LANES : (i + 1) * LANES]

    def strided(g, src, dst):
        matrix = gate(g)
        for pair in range(2):
            x = jnp.concatenate(
                [
                    jnp.concatenate([src[part, pl.ds(2 * pair + c, ORDER, stride=4), :] for part in range(2)], 0)
                    for c in range(2)
                ],
                1,
            )
            y = left(matrix, x)
            for c in range(2):
                for part in range(2):
                    dst[part, pl.ds(2 * pair + c, ORDER, stride=4), :] = y[
                        part * ORDER : (part + 1) * ORDER, c * LANES : (c + 1) * LANES
                    ]

    def halves_of(g, k):
        arrive(g % distinct)
        prepare_halves(g_ref, gh, k, g % distinct)

    def strided_half(k, src, dst, h, add):
        matrix = gh[k, h]
        base = pl.multiple_of(h * (rows // 2), rows // 2)
        for pair in range(2):
            x = jnp.concatenate(
                [
                    jnp.concatenate(
                        [src[part, pl.ds(base + 2 * pair + c, ORDER // 2, stride=4), :] for part in range(2)], 0
                    )
                    for c in range(2)
                ],
                1,
            )
            y = left(matrix, x)
            for c in range(2):
                for part in range(2):
                    z = y[part * ORDER : (part + 1) * ORDER, c * LANES : (c + 1) * LANES]
                    some = pl.ds(2 * pair + c, ORDER, stride=4)
                    if add:
                        z = z + dst[part, some, :]
                    dst[part, some, :] = z

    def middle(g, y):
        return swap_blocks(left(gate(g), swap_blocks(y)))

    def low_gates(x):
        y = to_right(middle(5, to_left(right(gate(4), x))))
        return right(gate(8), y)

    halves = [(0, quarter, 2 * quarter, 3 * quarter)]
    gate(0)
    gate(1)
    for a in range(QUARTERS):
        load_x(a).wait()
    x = jnp.concatenate([x_ref[pl.ds(part, rows, stride=2), :] for part in range(2)], 1)
    store(sa, 0, to_right(middle(1, to_left(right(gate(0), x)))))
    gate(2)
    gate(3)
    strided(2, sa, sb)
    pl.semaphore_wait(barrier, nodes - 1)

    slot = reversed3(me & 7)
    part1 = rows // 8
    copies = []
    for orders in ((1,), (0,), (3, 2)):
        spots = [(slot >> 1) ^ order for order in orders]
        firsts = [pl.multiple_of(a * quarter, quarter) for a in spots]
        y = left(gate(3), load_quarters(sb, firsts))
        if max(orders) < 2:
            store_quarters(sc, firsts, y)
        else:
            y = low_gates(to_right(y))
            for i, first in enumerate(firsts):
                store(sc, first, y[i * quarter : (i + 1) * quarter])
        for order, a, low in [(order, a, low) for order, a in zip(orders, spots) for low in (1, 0)]:
            if order == 0 and low == 0:
                mine = pl.ds(pl.multiple_of(slot * part1, part1), part1)
                r1[:, mine, :] = sc[:, mine, :]
                continue
            block = 2 * a + ((slot & 1) ^ low)
            index = 2 * order + low
            copy = pltpu.make_async_remote_copy(
                src_ref=sc.at[:, pl.ds(pl.multiple_of(block * part1, part1), part1), :],
                dst_ref=r1.at[:, pl.ds(pl.multiple_of(slot * part1, part1), part1), :],
                send_sem=send1.at[index],
                recv_sem=recv1.at[index],
                device_id={"node": (me & ~7) | reversed3(block)},
                device_id_type=pl.DeviceIdType.MESH,
            )
            copy.start()
            copies.append((index, copy))

    halves_of(6, 0)
    gate(7)
    gate(9)

    arrivals = dict(copies)
    firsts = []
    for index in range(4):
        if index in arrivals:
            arrivals[index].wait_recv()
        firsts.append(pl.multiple_of((slot ^ index) * part1, part1))
    x = jnp.concatenate(
        [jnp.concatenate([r1[part, pl.ds(first, part1), :] for part in range(2)], 1) for first in firsts], 0
    )
    y = low_gates(x)
    for i, first in enumerate(firsts):
        store(sa, first, y[i * part1 : (i + 1) * part1])
    strided_half(0, sa, sb, slot >> 2, False)
    for index in range(4, 8):
        arrivals[index].wait_recv()
    strided_half(0, r1, sb, (slot >> 2) ^ 1, True)

    part2 = rows // nodes
    per = nodes // QUARTERS
    early = part2 * LANES >= 1 << 11
    second = []
    mine = pl.ds(pl.multiple_of(me * part2, part2), part2)
    for orders in ((2,), (3, 1), (0,)):
        firsts = [pl.multiple_of(((me // per) ^ order) * quarter, quarter) for order in orders]
        y = left(gate(7), load_quarters(sb, firsts))
        if early:
            y = middle(9, y)
        store_quarters(sd, firsts, y)
        for order, low in [(order, low) for order in orders for low in range(per - 1, -1, -1)]:
            if order == 0 and low == 0:
                r2[:, mine, :] = sd[:, mine, :]
                continue
            block = me ^ (order * per + low)
            index = order * per + low
            copy = pltpu.make_async_remote_copy(
                src_ref=sd.at[:, pl.ds(pl.multiple_of(block * part2, part2), part2), :],
                dst_ref=r2.at[:, mine, :],
                send_sem=send2.at[index],
                recv_sem=recv2.at[index],
                device_id={"node": block},
                device_id_type=pl.DeviceIdType.MESH,
            )
            copy.start()
            second.append((index, copy))

    halves_of(10, 1)
    gate(11)
    for _, copy in copies:
        copy.wait_send()
    side = me // (nodes // 2)
    if early:
        for far in range(2):
            for index, copy in second:
                if index // (nodes // 2) == far:
                    copy.wait_recv()
            strided_half(1, r2, sa, side ^ far, far == 1)
    else:
        for _, copy in second:
            copy.wait_recv()
        for firsts in halves:
            store_quarters(sb, firsts, middle(9, load_quarters(r2, firsts)))
        for far in range(2):
            strided_half(1, sb, sa, side ^ far, far == 1)
    for firsts in halves:
        y = left(gate(11), load_quarters(sa, firsts))
        for i, first in enumerate(firsts):
            for part in range(2):
                o_ref[pl.ds(2 * first + part, quarter, stride=2), :] = y[
                    part * ORDER : (part + 1) * ORDER, i * LANES : (i + 1) * LANES
                ]
    for _, copy in second:
        copy.wait_send()


def body(nodes, amplitudes, gates):
    total = amplitudes.shape[1]
    distinct = gates.shape[1]
    rows = total // LANES
    x = amplitudes.reshape(2, rows, LANES).transpose(1, 0, 2).reshape(2 * rows, LANES)
    state = pltpu.VMEM((2, rows, LANES), F32)
    out = pl.pallas_call(
        functools.partial(kernel, nodes, distinct),
        out_shape=jax.ShapeDtypeStruct((2 * rows, LANES), F32),
        in_specs=[pl.BlockSpec(memory_space=pltpu.HBM)] * 2,
        out_specs=pl.BlockSpec(memory_space=pltpu.VMEM),
        scratch_shapes=[
            pltpu.VMEM((2 * rows, LANES), F32),
            pltpu.VMEM(gates.shape, F32),
            pltpu.VMEM((distinct, 2 * ORDER, 6 * ORDER), BF16),
            pltpu.VMEM((2, 2, 2 * ORDER, 3 * ORDER), BF16),
            state,
            state,
            state,
            state,
            state,
            state,
            pltpu.SemaphoreType.DMA((QUARTERS,)),
            pltpu.SemaphoreType.DMA((distinct,)),
            pltpu.SemaphoreType.DMA((8,)),
            pltpu.SemaphoreType.DMA((8,)),
            pltpu.SemaphoreType.DMA((nodes,)),
            pltpu.SemaphoreType.DMA((nodes,)),
        ],
        compiler_params=pltpu.CompilerParams(collective_id=0, has_side_effects=True, vmem_limit_bytes=53 << 20),
        name="circuit",
    )(x, gates)
    return out.reshape(rows, 2, LANES).transpose(1, 0, 2).reshape(2, total)


def solution(mesh):
    spec = P(None, ("paths", "node"))
    return jax.shard_map(
        functools.partial(body, mesh.shape["node"]), mesh=mesh, in_specs=(spec, P()), out_specs=spec, check_vma=False
    )
```

```python
import functools

import jax
import jax.numpy as jnp
from jax import lax
from jax.experimental import pallas as pl
from jax.experimental.pallas import tpu as pltpu
from jax.sharding import PartitionSpec as P

F32 = jnp.float32
BF16 = jnp.bfloat16
ORDER = 128
LANES = 128
QUARTERS = 4


def split(x):
    high = x.astype(BF16)
    low = (x - high.astype(F32)).astype(BF16)
    return high, low


def exchange_bits(groups):
    lane = lax.broadcasted_iota(jnp.int32, groups[0].shape, 1)
    turned = [groups[0]] + [pltpu.roll(groups[i], 16 * i, 1) for i in range(1, 8)]
    turned = [turned[-i % 8] for i in range(8)]
    for k in range(3):
        here = (lane & (16 << k)) == 0
        turned = [jnp.where(here, turned[i], turned[(i - (1 << k)) % 8]) for i in range(8)]
    return [turned[0]] + [pltpu.roll(turned[i], LANES - 16 * i, 1) for i in range(1, 8)]


def swap_blocks(y):
    columns = []
    for start in range(0, y.shape[1], LANES):
        parts = []
        for base in range(0, 2 * ORDER, ORDER):
            parts += exchange_bits(
                [y[base + 16 * i : base + 16 * i + 16, start : start + LANES] for i in range(8)]
            )
        columns.append(jnp.concatenate(parts, 0))
    return jnp.concatenate(columns, 1)


def to_left(y):
    return jnp.concatenate(
        [
            jnp.concatenate([y[i : i + ORDER, :LANES], y[i : i + ORDER, LANES:]], 0)
            for i in range(0, y.shape[0], ORDER)
        ],
        1,
    )


def to_right(y):
    return jnp.concatenate(
        [
            jnp.concatenate([y[:ORDER, i : i + LANES], y[ORDER:, i : i + LANES]], 1)
            for i in range(0, y.shape[1], LANES)
        ],
        0,
    )


def prepare(g_ref, gc_ref, m, permuted):
    real_high, real_low = split(g_ref[0, m])
    imag_high, imag_low = split(g_ref[1, m])
    blocks = [real_high, real_low, imag_high, imag_low]
    if permuted:
        row = lax.broadcasted_iota(jnp.int32, (ORDER, ORDER), 0)
        column = lax.broadcasted_iota(jnp.int32, (ORDER, ORDER), 1)
        place = ((row & 15) << 3) + (row >> 4)
        move = jnp.where(column == place, 1.0, 0.0).astype(BF16)
        wide = jnp.dot(move, jnp.concatenate(blocks, 1), preferred_element_type=F32).astype(BF16)
        blocks = [
            lax.dot_general(
                wide[:, i * ORDER : (i + 1) * ORDER], move, (((1,), (1,)), ((), ())), preferred_element_type=F32
            ).astype(BF16)
            for i in range(4)
        ]
    real_high, real_low, imag_high, imag_low = blocks
    gc_ref[m, :ORDER, :] = jnp.concatenate([real_high, -imag_high, real_low, -imag_low, real_high, -imag_high], 1)
    gc_ref[m, ORDER:, :] = jnp.concatenate([imag_high, real_high, imag_low, real_low, imag_high, real_high], 1)


def prepare_halves(g_ref, gh_ref, k, m):
    real, imag = g_ref[0, m], g_ref[1, m]
    half = ORDER // 2
    below = lax.broadcasted_iota(jnp.int32, (ORDER, ORDER), 1) < half

    def fold(a, b):
        return jnp.where(below, a, pltpu.roll(b, half, 1)), jnp.where(below, pltpu.roll(a, half, 1), b)

    for part, sides in enumerate((fold(real, -imag), fold(imag, real))):
        for h in range(2):
            high, low = split(sides[h])
            gh_ref[k, h, part * ORDER : (part + 1) * ORDER, :] = jnp.concatenate([high, low, high], 1)


def left(gate, x):
    high, low = split(x)
    return jnp.dot(gate, jnp.concatenate([high, high, low], 0), preferred_element_type=F32)


def right(gate, x):
    high, low = split(x)
    return lax.dot_general(
        jnp.concatenate([high, high, low], 1), gate, (((1,), (1,)), ((), ())), preferred_element_type=F32
    )


def reversed3(x):
    return ((x & 1) << 2) | (x & 2) | ((x >> 2) & 1)


def kernel(
    nodes, distinct, x_hbm, g_hbm, o_ref, x_ref, g_ref, gc, gh, sa, sb, sc, sd, r1, r2, in_x, in_g, send1, recv1, send2, recv2
):
    rows = sa.shape[1]
    quarter = rows // QUARTERS

    def load_x(a):
        some = pl.ds(2 * a * quarter, 2 * quarter)
        return pltpu.make_async_copy(x_hbm.at[some, :], x_ref.at[some, :], in_x.at[a])

    def load_gate(m):
        return pltpu.make_async_copy(g_hbm.at[:, m], g_ref.at[:, m], in_g.at[m])

    sequence = list(dict.fromkeys(g % distinct for g in (0, 1, 2, 3, 4, 5, 8, 6, 7, 9, 10, 11)))
    for m in sequence[:2]:
        load_gate(m).start()
    for a in range(QUARTERS):
        load_x(a).start()
    for m in sequence[2:]:
        load_gate(m).start()
    me = lax.axis_index("node")
    barrier = pltpu.get_barrier_semaphore()
    for i in range(1, nodes):
        pl.semaphore_signal(barrier, inc=1, device_id={"node": me ^ i}, device_id_type=pl.DeviceIdType.MESH)

    ready = set()
    loaded = set()

    def arrive(m):
        if m not in loaded:
            loaded.add(m)
            load_gate(m).wait()

    def gate(g):
        m = g % distinct
        if m not in ready:
            ready.add(m)
            arrive(m)
            prepare(g_ref, gc, m, g % 4 == 1)
        return gc[m]

    def store(ref, first, y):
        ref[0, pl.ds(first, y.shape[0]), :] = y[:, :LANES]
        ref[1, pl.ds(first, y.shape[0]), :] = y[:, LANES:]

    def load_quarters(ref, firsts):
        return jnp.concatenate(
            [
                jnp.concatenate([ref[0, pl.ds(first, quarter), :], ref[1, pl.ds(first, quarter), :]], 0)
                for first in firsts
            ],
            1,
        )

    def store_quarters(ref, firsts, y):
        for i, first in enumerate(firsts):
            ref[0, pl.ds(first, quarter), :] = y[:ORDER, i * LANES : (i + 1) * LANES]
            ref[1, pl.ds(first, quarter), :] = y[ORDER:, i * LANES : (i + 1) * LANES]

    def strided(g, src, dst):
        matrix = gate(g)
        for pair in range(2):
            x = jnp.concatenate(
                [
                    jnp.concatenate([src[part, pl.ds(2 * pair + c, ORDER, stride=4), :] for part in range(2)], 0)
                    for c in range(2)
                ],
                1,
            )
            y = left(matrix, x)
            for c in range(2):
                for part in range(2):
                    dst[part, pl.ds(2 * pair + c, ORDER, stride=4), :] = y[
                        part * ORDER : (part + 1) * ORDER, c * LANES : (c + 1) * LANES
                    ]

    def halves_of(g, k):
        arrive(g % distinct)
        prepare_halves(g_ref, gh, k, g % distinct)

    def strided_half(k, src, dst, h, add):
        matrix = gh[k, h]
        base = pl.multiple_of(h * (rows // 2), rows // 2)
        for pair in range(2):
            x = jnp.concatenate(
                [
                    jnp.concatenate(
                        [src[part, pl.ds(base + 2 * pair + c, ORDER // 2, stride=4), :] for part in range(2)], 0
                    )
                    for c in range(2)
                ],
                1,
            )
            y = left(matrix, x)
            for c in range(2):
                for part in range(2):
                    z = y[part * ORDER : (part + 1) * ORDER, c * LANES : (c + 1) * LANES]
                    some = pl.ds(2 * pair + c, ORDER, stride=4)
                    if add:
                        z = z + dst[part, some, :]
                    dst[part, some, :] = z

    def middle(g, y):
        return swap_blocks(left(gate(g), swap_blocks(y)))

    def low_gates(x):
        y = to_right(middle(5, to_left(right(gate(4), x))))
        return right(gate(8), y)

    halves = [(0, quarter, 2 * quarter, 3 * quarter)]
    gate(0)
    gate(1)
    for a in range(QUARTERS):
        load_x(a).wait()
    x = jnp.concatenate([x_ref[pl.ds(part, rows, stride=2), :] for part in range(2)], 1)
    store(sa, 0, to_right(middle(1, to_left(right(gate(0), x)))))
    gate(2)
    gate(3)
    strided(2, sa, sb)
    pl.semaphore_wait(barrier, nodes - 1)

    slot = reversed3(me & 7)
    part1 = rows // 8
    copies = []
    for orders in ((1,), (0,), (3, 2)):
        spots = [(slot >> 1) ^ order for order in orders]
        firsts = [pl.multiple_of(a * quarter, quarter) for a in spots]
        y = left(gate(3), load_quarters(sb, firsts))
        if max(orders) < 2:
            store_quarters(sc, firsts, y)
        else:
            y = low_gates(to_right(y))
            for i, first in enumerate(firsts):
                store(sc, first, y[i * quarter : (i + 1) * quarter])
        for order, a, low in [(order, a, low) for order, a in zip(orders, spots) for low in (1, 0)]:
            if order == 0 and low == 0:
                mine = pl.ds(pl.multiple_of(slot * part1, part1), part1)
                r1[:, mine, :] = sc[:, mine, :]
                continue
            block = 2 * a + ((slot & 1) ^ low)
            index = 2 * order + low
            copy = pltpu.make_async_remote_copy(
                src_ref=sc.at[:, pl.ds(pl.multiple_of(block * part1, part1), part1), :],
                dst_ref=r1.at[:, pl.ds(pl.multiple_of(slot * part1, part1), part1), :],
                send_sem=send1.at[index],
                recv_sem=recv1.at[index],
                device_id={"node": (me & ~7) | reversed3(block)},
                device_id_type=pl.DeviceIdType.MESH,
            )
            copy.start()
            copies.append((index, copy))

    halves_of(6, 0)
    gate(7)
    gate(9)

    arrivals = dict(copies)
    firsts = []
    for index in range(4):
        if index in arrivals:
            arrivals[index].wait_recv()
        firsts.append(pl.multiple_of((slot ^ index) * part1, part1))
    x = jnp.concatenate(
        [jnp.concatenate([r1[part, pl.ds(first, part1), :] for part in range(2)], 1) for first in firsts], 0
    )
    y = low_gates(x)
    for i, first in enumerate(firsts):
        store(sa, first, y[i * part1 : (i + 1) * part1])
    strided_half(0, sa, sb, slot >> 2, False)
    for index in range(4, 8):
        arrivals[index].wait_recv()
    strided_half(0, r1, sb, (slot >> 2) ^ 1, True)

    part2 = rows // nodes
    per = nodes // QUARTERS
    early = part2 * LANES >= 1 << 11
    mine = pl.ds(pl.multiple_of(me * part2, part2), part2)
    spot = me // per
    even = 1 - (spot & 1)
    side = me // (nodes // 2)

    def second(index):
        block = me ^ index
        return pltpu.make_async_remote_copy(
            src_ref=sd.at[:, pl.ds(pl.multiple_of(block * part2, part2), part2), :],
            dst_ref=r2.at[:, mine, :],
            send_sem=send2.at[index],
            recv_sem=recv2.at[index],
            device_id={"node": block},
            device_id_type=pl.DeviceIdType.MESH,
        )

    for phase, orders in enumerate(((3 - even,), (1, 2 + even), (0,))):
        firsts = [pl.multiple_of((spot ^ order) * quarter, quarter) for order in orders]
        y = left(gate(7), load_quarters(sb, firsts))
        if early and phase > 0:
            y = middle(9, y)
        store_quarters(sd, firsts, y)
        for order, low in [(order, low) for order in orders for low in range(per - 1, -1, -1)]:
            if isinstance(order, int) and order == 0 and low == 0:
                r2[:, mine, :] = sd[:, mine, :]
            else:
                second(order * per + low).start()

    halves_of(10, 1)
    gate(11)
    for _, copy in copies:
        copy.wait_send()
    if early:

        def arrive_half(far):
            for low in range(1, nodes // 2):
                second(far * (nodes // 2) + low).wait_recv()

            @pl.when(far == 1)
            def _():
                second(nodes // 2).wait_recv()

        arrive_half(even)

        @pl.when(even == 1)
        def _():
            firsts = [pl.multiple_of((spot ^ order) * quarter, quarter) for order in (2, 3)]
            store_quarters(r2, firsts, middle(9, load_quarters(r2, firsts)))

        strided_half(1, r2, sa, side ^ even, False)
        arrive_half(1 - even)
        strided_half(1, r2, sa, side ^ (1 - even), True)
    else:
        for index in range(1, nodes):
            second(index).wait_recv()
        for firsts in halves:
            store_quarters(sb, firsts, middle(9, load_quarters(r2, firsts)))
        for far in range(2):
            strided_half(1, sb, sa, side ^ far, far == 1)
    for firsts in halves:
        y = left(gate(11), load_quarters(sa, firsts))
        for i, first in enumerate(firsts):
            for part in range(2):
                o_ref[pl.ds(2 * first + part, quarter, stride=2), :] = y[
                    part * ORDER : (part + 1) * ORDER, i * LANES : (i + 1) * LANES
                ]
    for index in range(1, nodes):
        second(index).wait_send()


def body(nodes, amplitudes, gates):
    total = amplitudes.shape[1]
    distinct = gates.shape[1]
    rows = total // LANES
    x = amplitudes.reshape(2, rows, LANES).transpose(1, 0, 2).reshape(2 * rows, LANES)
    state = pltpu.VMEM((2, rows, LANES), F32)
    out = pl.pallas_call(
        functools.partial(kernel, nodes, distinct),
        out_shape=jax.ShapeDtypeStruct((2 * rows, LANES), F32),
        in_specs=[pl.BlockSpec(memory_space=pltpu.HBM)] * 2,
        out_specs=pl.BlockSpec(memory_space=pltpu.VMEM),
        scratch_shapes=[
            pltpu.VMEM((2 * rows, LANES), F32),
            pltpu.VMEM(gates.shape, F32),
            pltpu.VMEM((distinct, 2 * ORDER, 6 * ORDER), BF16),
            pltpu.VMEM((2, 2, 2 * ORDER, 3 * ORDER), BF16),
            state,
            state,
            state,
            state,
            state,
            state,
            pltpu.SemaphoreType.DMA((QUARTERS,)),
            pltpu.SemaphoreType.DMA((distinct,)),
            pltpu.SemaphoreType.DMA((8,)),
            pltpu.SemaphoreType.DMA((8,)),
            pltpu.SemaphoreType.DMA((nodes,)),
            pltpu.SemaphoreType.DMA((nodes,)),
        ],
        compiler_params=pltpu.CompilerParams(collective_id=0, has_side_effects=True, vmem_limit_bytes=53 << 20),
        name="circuit",
    )(x, gates)
    return out.reshape(rows, 2, LANES).transpose(1, 0, 2).reshape(2, total)


def solution(mesh):
    spec = P(None, ("paths", "node"))
    return jax.shard_map(
        functools.partial(body, mesh.shape["node"]), mesh=mesh, in_specs=(spec, P()), out_specs=spec, check_vma=False
    )
```

```python
import functools

import jax
import jax.numpy as jnp
from jax import lax
from jax.experimental import pallas as pl
from jax.experimental.pallas import tpu as pltpu
from jax.sharding import PartitionSpec as P

F32 = jnp.float32
BF16 = jnp.bfloat16
ORDER = 128
LANES = 128
QUARTERS = 4
GROUPS = (0, 2, 4, 6)


def split(x):
    high = x.astype(BF16)
    low = (x - high.astype(F32)).astype(BF16)
    return high, low


def exchange_bits(groups):
    lane = lax.broadcasted_iota(jnp.int32, groups[0].shape, 1)
    turned = [groups[0]] + [pltpu.roll(groups[i], 16 * i, 1) for i in range(1, 8)]
    turned = [turned[-i % 8] for i in range(8)]
    for k in range(3):
        here = (lane & (16 << k)) == 0
        turned = [jnp.where(here, turned[i], turned[(i - (1 << k)) % 8]) for i in range(8)]
    return [turned[0]] + [pltpu.roll(turned[i], LANES - 16 * i, 1) for i in range(1, 8)]


def swap_blocks(y):
    columns = []
    for start in range(0, y.shape[1], LANES):
        parts = []
        for base in range(0, 2 * ORDER, ORDER):
            parts += exchange_bits(
                [y[base + 16 * i : base + 16 * i + 16, start : start + LANES] for i in range(8)]
            )
        columns.append(jnp.concatenate(parts, 0))
    return jnp.concatenate(columns, 1)


def to_left(y):
    return jnp.concatenate(
        [
            jnp.concatenate([y[i : i + ORDER, :LANES], y[i : i + ORDER, LANES:]], 0)
            for i in range(0, y.shape[0], ORDER)
        ],
        1,
    )


def to_right(y):
    return jnp.concatenate(
        [
            jnp.concatenate([y[:ORDER, i : i + LANES], y[ORDER:, i : i + LANES]], 1)
            for i in range(0, y.shape[1], LANES)
        ],
        0,
    )


def prepare(g_ref, gc_ref, m, permuted):
    real_high, real_low = split(g_ref[0, m])
    imag_high, imag_low = split(g_ref[1, m])
    blocks = [real_high, real_low, imag_high, imag_low]
    if permuted:
        row = lax.broadcasted_iota(jnp.int32, (ORDER, ORDER), 0)
        column = lax.broadcasted_iota(jnp.int32, (ORDER, ORDER), 1)
        place = ((row & 15) << 3) + (row >> 4)
        move = jnp.where(column == place, 1.0, 0.0).astype(BF16)
        wide = jnp.dot(move, jnp.concatenate(blocks, 1), preferred_element_type=F32).astype(BF16)
        blocks = [
            lax.dot_general(
                wide[:, i * ORDER : (i + 1) * ORDER], move, (((1,), (1,)), ((), ())), preferred_element_type=F32
            ).astype(BF16)
            for i in range(4)
        ]
    real_high, real_low, imag_high, imag_low = blocks
    gc_ref[m, :ORDER, :] = jnp.concatenate([real_high, -imag_high, real_low, -imag_low, real_high, -imag_high], 1)
    gc_ref[m, ORDER:, :] = jnp.concatenate([imag_high, real_high, imag_low, real_low, imag_high, real_high], 1)


def prepare_halves(g_ref, gh_ref, k, m):
    real, imag = g_ref[0, m], g_ref[1, m]
    half = ORDER // 2
    below = lax.broadcasted_iota(jnp.int32, (ORDER, ORDER), 1) < half

    def fold(a, b):
        return jnp.where(below, a, pltpu.roll(b, half, 1)), jnp.where(below, pltpu.roll(a, half, 1), b)

    for part, sides in enumerate((fold(real, -imag), fold(imag, real))):
        for h in range(2):
            high, low = split(sides[h])
            gh_ref[k, h, part * ORDER : (part + 1) * ORDER, :] = jnp.concatenate([high, low, high], 1)


def left(gate, x):
    high, low = split(x)
    return jnp.dot(gate, jnp.concatenate([high, high, low], 0), preferred_element_type=F32)


def right(gate, x):
    high, low = split(x)
    return lax.dot_general(
        jnp.concatenate([high, high, low], 1), gate, (((1,), (1,)), ((), ())), preferred_element_type=F32
    )


def reversed3(x):
    return ((x & 1) << 2) | (x & 2) | ((x >> 2) & 1)


def kernel(
    nodes, distinct, x_hbm, g_hbm, o_ref, x_ref, g_ref, gc, gh, sa, sb, sc, sd, r1, r2, in_x, in_g, send1, recv1, send2, recv2
):
    rows = sa.shape[1]
    quarter = rows // QUARTERS

    load_x = pltpu.make_async_copy(x_hbm, x_ref, in_x.at[0])
    bounds = (*GROUPS, distinct)

    def load_gates(i):
        some = pl.ds(bounds[i], bounds[i + 1] - bounds[i])
        return pltpu.make_async_copy(g_hbm.at[:, some], g_ref.at[:, some], in_g.at[i])

    load_gates(0).start()
    load_x.start()
    for i in range(1, len(GROUPS)):
        load_gates(i).start()
    me = lax.axis_index("node")
    barrier = pltpu.get_barrier_semaphore()
    for i in range(1, nodes):
        pl.semaphore_signal(barrier, inc=1, device_id={"node": me ^ i}, device_id_type=pl.DeviceIdType.MESH)

    ready = set()
    loaded = set()

    def arrive(m):
        i = sum(m >= bound for bound in GROUPS) - 1
        if i not in loaded:
            loaded.add(i)
            load_gates(i).wait()

    def gate(g):
        m = g % distinct
        if m not in ready:
            ready.add(m)
            arrive(m)
            prepare(g_ref, gc, m, g % 4 == 1)
        return gc[m]

    def store(ref, first, y):
        ref[0, pl.ds(first, y.shape[0]), :] = y[:, :LANES]
        ref[1, pl.ds(first, y.shape[0]), :] = y[:, LANES:]

    def load_quarters(ref, firsts):
        return jnp.concatenate(
            [
                jnp.concatenate([ref[0, pl.ds(first, quarter), :], ref[1, pl.ds(first, quarter), :]], 0)
                for first in firsts
            ],
            1,
        )

    def store_quarters(ref, firsts, y):
        for i, first in enumerate(firsts):
            ref[0, pl.ds(first, quarter), :] = y[:ORDER, i * LANES : (i + 1) * LANES]
            ref[1, pl.ds(first, quarter), :] = y[ORDER:, i * LANES : (i + 1) * LANES]

    def strided(g, src, dst):
        matrix = gate(g)
        for pair in range(2):
            x = jnp.concatenate(
                [
                    jnp.concatenate([src[part, pl.ds(2 * pair + c, ORDER, stride=4), :] for part in range(2)], 0)
                    for c in range(2)
                ],
                1,
            )
            y = left(matrix, x)
            for c in range(2):
                for part in range(2):
                    dst[part, pl.ds(2 * pair + c, ORDER, stride=4), :] = y[
                        part * ORDER : (part + 1) * ORDER, c * LANES : (c + 1) * LANES
                    ]

    def finish(ref, some, sem):
        pltpu.make_async_copy(ref.at[:, pl.ds(0, some), :], ref.at[:, pl.ds(0, some), :], sem).wait()

    def halves_of(g, k):
        arrive(g % distinct)
        prepare_halves(g_ref, gh, k, g % distinct)

    def strided_half(k, src, dst, h, add):
        matrix = gh[k, h]
        base = pl.multiple_of(h * (rows // 2), rows // 2)
        for pair in range(2):
            x = jnp.concatenate(
                [
                    jnp.concatenate(
                        [src[part, pl.ds(base + 2 * pair + c, ORDER // 2, stride=4), :] for part in range(2)], 0
                    )
                    for c in range(2)
                ],
                1,
            )
            y = left(matrix, x)
            for c in range(2):
                for part in range(2):
                    z = y[part * ORDER : (part + 1) * ORDER, c * LANES : (c + 1) * LANES]
                    some = pl.ds(2 * pair + c, ORDER, stride=4)
                    if add:
                        z = z + dst[part, some, :]
                    dst[part, some, :] = z

    def middle(g, y):
        return swap_blocks(left(gate(g), swap_blocks(y)))

    def low_gates(x):
        y = to_right(middle(5, to_left(right(gate(4), x))))
        return right(gate(8), y)

    halves = [(0, quarter, 2 * quarter, 3 * quarter)]
    gate(0)
    gate(1)
    load_x.wait()
    x = jnp.concatenate([x_ref[pl.ds(part, rows, stride=2), :] for part in range(2)], 1)
    store(sa, 0, to_right(middle(1, to_left(right(gate(0), x)))))
    gate(2)
    gate(3)
    strided(2, sa, sb)
    pl.semaphore_wait(barrier, nodes - 1)

    slot = reversed3(me & 7)
    part1 = rows // 8
    for orders in ((1,), (0,), (3, 2)):
        spots = [(slot >> 1) ^ order for order in orders]
        firsts = [pl.multiple_of(a * quarter, quarter) for a in spots]
        y = left(gate(3), load_quarters(sb, firsts))
        if max(orders) < 2:
            store_quarters(sc, firsts, y)
        else:
            y = low_gates(to_right(y))
            for i, first in enumerate(firsts):
                store(sc, first, y[i * quarter : (i + 1) * quarter])
        for order, a, low in [(order, a, low) for order, a in zip(orders, spots) for low in (1, 0)]:
            if order == 0 and low == 0:
                mine = pl.ds(pl.multiple_of(slot * part1, part1), part1)
                r1[:, mine, :] = sc[:, mine, :]
                continue
            block = 2 * a + ((slot & 1) ^ low)
            index = 2 * order + low
            pltpu.make_async_remote_copy(
                src_ref=sc.at[:, pl.ds(pl.multiple_of(block * part1, part1), part1), :],
                dst_ref=r1.at[:, pl.ds(pl.multiple_of(slot * part1, part1), part1), :],
                send_sem=send1.at[0],
                recv_sem=recv1.at[index // 4],
                device_id={"node": (me & ~7) | reversed3(block)},
                device_id_type=pl.DeviceIdType.MESH,
            ).start()

    halves_of(6, 0)
    gate(7)
    gate(9)

    finish(r1, 3 * part1, recv1.at[0])
    firsts = [pl.multiple_of((slot ^ index) * part1, part1) for index in range(4)]
    x = jnp.concatenate(
        [jnp.concatenate([r1[part, pl.ds(first, part1), :] for part in range(2)], 1) for first in firsts], 0
    )
    y = low_gates(x)
    for i, first in enumerate(firsts):
        store(sa, first, y[i * part1 : (i + 1) * part1])
    strided_half(0, sa, sb, slot >> 2, False)
    finish(r1, 4 * part1, recv1.at[1])
    strided_half(0, r1, sb, (slot >> 2) ^ 1, True)

    part2 = rows // nodes
    per = nodes // QUARTERS
    early = part2 * LANES >= 1 << 11
    mine = pl.ds(pl.multiple_of(me * part2, part2), part2)
    spot = me // per
    even = 1 - (spot & 1)
    side = me // (nodes // 2)

    def second(index, far):
        block = me ^ index
        return pltpu.make_async_remote_copy(
            src_ref=sd.at[:, pl.ds(pl.multiple_of(block * part2, part2), part2), :],
            dst_ref=r2.at[:, mine, :],
            send_sem=send2.at[0],
            recv_sem=recv2.at[far],
            device_id={"node": block},
            device_id_type=pl.DeviceIdType.MESH,
        )

    for phase, orders in enumerate(((3 - even,), (1, 2 + even), (0,))):
        firsts = [pl.multiple_of((spot ^ order) * quarter, quarter) for order in orders]
        y = left(gate(7), load_quarters(sb, firsts))
        if early and phase > 0:
            y = middle(9, y)
        store_quarters(sd, firsts, y)
        for order, low in [(order, low) for order in orders for low in range(per - 1, -1, -1)]:
            if isinstance(order, int) and order == 0 and low == 0:
                r2[:, mine, :] = sd[:, mine, :]
            else:
                second(order * per + low, 0 if isinstance(order, int) and order < 2 else 1).start()

    halves_of(10, 1)
    gate(11)
    finish(sc, 7 * part1, send1.at[0])

    def arrive_half(far):
        finish(r2, (nodes // 2 - 1 + far) * part2, recv2.at[far])

    if early:

        @pl.when(even == 0)
        def _():
            arrive_half(0)

        @pl.when(even == 1)
        def _():
            arrive_half(1)
            firsts = [pl.multiple_of((spot ^ order) * quarter, quarter) for order in (2, 3)]
            store_quarters(r2, firsts, middle(9, load_quarters(r2, firsts)))

        strided_half(1, r2, sa, side ^ even, False)

        @pl.when(even == 0)
        def _():
            arrive_half(1)

        @pl.when(even == 1)
        def _():
            arrive_half(0)

        strided_half(1, r2, sa, side ^ (1 - even), True)
    else:
        arrive_half(0)
        arrive_half(1)
        for firsts in halves:
            store_quarters(sb, firsts, middle(9, load_quarters(r2, firsts)))
        for far in range(2):
            strided_half(1, sb, sa, side ^ far, far == 1)
    for firsts in halves:
        y = left(gate(11), load_quarters(sa, firsts))
        for i, first in enumerate(firsts):
            for part in range(2):
                o_ref[pl.ds(2 * first + part, quarter, stride=2), :] = y[
                    part * ORDER : (part + 1) * ORDER, i * LANES : (i + 1) * LANES
                ]
    finish(sd, (nodes - 1) * part2, send2.at[0])


def body(nodes, amplitudes, gates):
    total = amplitudes.shape[1]
    distinct = gates.shape[1]
    rows = total // LANES
    x = amplitudes.reshape(2, rows, LANES).transpose(1, 0, 2).reshape(2 * rows, LANES)
    state = pltpu.VMEM((2, rows, LANES), F32)
    out = pl.pallas_call(
        functools.partial(kernel, nodes, distinct),
        out_shape=jax.ShapeDtypeStruct((2 * rows, LANES), F32),
        in_specs=[pl.BlockSpec(memory_space=pltpu.HBM)] * 2,
        out_specs=pl.BlockSpec(memory_space=pltpu.VMEM),
        scratch_shapes=[
            pltpu.VMEM((2 * rows, LANES), F32),
            pltpu.VMEM(gates.shape, F32),
            pltpu.VMEM((distinct, 2 * ORDER, 6 * ORDER), BF16),
            pltpu.VMEM((2, 2, 2 * ORDER, 3 * ORDER), BF16),
            state,
            state,
            state,
            state,
            state,
            state,
            pltpu.SemaphoreType.DMA((1,)),
            pltpu.SemaphoreType.DMA((len(GROUPS),)),
            pltpu.SemaphoreType.DMA((1,)),
            pltpu.SemaphoreType.DMA((2,)),
            pltpu.SemaphoreType.DMA((1,)),
            pltpu.SemaphoreType.DMA((2,)),
        ],
        compiler_params=pltpu.CompilerParams(collective_id=0, has_side_effects=True, vmem_limit_bytes=53 << 20),
        name="circuit",
    )(x, gates)
    return out.reshape(rows, 2, LANES).transpose(1, 0, 2).reshape(2, total)


def solution(mesh):
    spec = P(None, ("paths", "node"))
    return jax.shard_map(
        functools.partial(body, mesh.shape["node"]), mesh=mesh, in_specs=(spec, P()), out_specs=spec, check_vma=False
    )
```

```python
import functools

import jax
import jax.numpy as jnp
from jax import lax
from jax.experimental import pallas as pl
from jax.experimental.pallas import tpu as pltpu
from jax.sharding import PartitionSpec as P

F32 = jnp.float32
BF16 = jnp.bfloat16
ORDER = 128
LANES = 128
QUARTERS = 4
GROUPS = (0, 2, 4, 6)


def split(x):
    high = x.astype(BF16)
    low = (x - high.astype(F32)).astype(BF16)
    return high, low


def exchange_bits(groups):
    lane = lax.broadcasted_iota(jnp.int32, groups[0].shape, 1)
    turned = [groups[0]] + [pltpu.roll(groups[i], 16 * i, 1) for i in range(1, 8)]
    turned = [turned[-i % 8] for i in range(8)]
    for k in range(3):
        here = (lane & (16 << k)) == 0
        turned = [jnp.where(here, turned[i], turned[(i - (1 << k)) % 8]) for i in range(8)]
    return [turned[0]] + [pltpu.roll(turned[i], LANES - 16 * i, 1) for i in range(1, 8)]


def swap_blocks(y):
    columns = []
    for start in range(0, y.shape[1], LANES):
        parts = []
        for base in range(0, 2 * ORDER, ORDER):
            parts += exchange_bits(
                [y[base + 16 * i : base + 16 * i + 16, start : start + LANES] for i in range(8)]
            )
        columns.append(jnp.concatenate(parts, 0))
    return jnp.concatenate(columns, 1)


def to_left(y):
    return jnp.concatenate(
        [
            jnp.concatenate([y[i : i + ORDER, :LANES], y[i : i + ORDER, LANES:]], 0)
            for i in range(0, y.shape[0], ORDER)
        ],
        1,
    )


def to_right(y):
    return jnp.concatenate(
        [
            jnp.concatenate([y[:ORDER, i : i + LANES], y[ORDER:, i : i + LANES]], 1)
            for i in range(0, y.shape[1], LANES)
        ],
        0,
    )


def prepare(g_ref, gc_ref, m, permuted):
    real_high, real_low = split(g_ref[0, m])
    imag_high, imag_low = split(g_ref[1, m])
    blocks = [real_high, real_low, imag_high, imag_low]
    if permuted:
        row = lax.broadcasted_iota(jnp.int32, (ORDER, ORDER), 0)
        column = lax.broadcasted_iota(jnp.int32, (ORDER, ORDER), 1)
        place = ((row & 15) << 3) + (row >> 4)
        move = jnp.where(column == place, 1.0, 0.0).astype(BF16)
        wide = jnp.dot(move, jnp.concatenate(blocks, 1), preferred_element_type=F32).astype(BF16)
        blocks = [
            lax.dot_general(
                wide[:, i * ORDER : (i + 1) * ORDER], move, (((1,), (1,)), ((), ())), preferred_element_type=F32
            ).astype(BF16)
            for i in range(4)
        ]
    real_high, real_low, imag_high, imag_low = blocks
    gc_ref[m, :ORDER, :] = jnp.concatenate([real_high, -imag_high, real_low, -imag_low, real_high, -imag_high], 1)
    gc_ref[m, ORDER:, :] = jnp.concatenate([imag_high, real_high, imag_low, real_low, imag_high, real_high], 1)


def prepare_halves(g_ref, gh_ref, k, m):
    real, imag = g_ref[0, m], g_ref[1, m]
    half = ORDER // 2
    below = lax.broadcasted_iota(jnp.int32, (ORDER, ORDER), 1) < half

    def fold(a, b):
        return jnp.where(below, a, pltpu.roll(b, half, 1)), jnp.where(below, pltpu.roll(a, half, 1), b)

    for part, sides in enumerate((fold(real, -imag), fold(imag, real))):
        for h in range(2):
            high, low = split(sides[h])
            gh_ref[k, h, part * ORDER : (part + 1) * ORDER, :] = jnp.concatenate([high, low, high], 1)


def left(gate, x):
    high, low = split(x)
    return jnp.dot(gate, jnp.concatenate([high, high, low], 0), preferred_element_type=F32)


def right(gate, x):
    some = x.shape[0] // 2
    return jnp.concatenate([right_rows(gate, x[:some]), right_rows(gate, x[some:])], 0)


def right_rows(gate, x):
    high, low = split(x)
    return lax.dot_general(
        jnp.concatenate([high, high, low], 1), gate, (((1,), (1,)), ((), ())), preferred_element_type=F32
    )


def reversed3(x):
    return ((x & 1) << 2) | (x & 2) | ((x >> 2) & 1)


def kernel(
    nodes, distinct, x_hbm, g_hbm, o_ref, x_ref, g_ref, gc, gh, sa, sb, sc, sd, r1, r2, in_x, in_g, send1, recv1, send2, recv2
):
    rows = sa.shape[1]
    quarter = rows // QUARTERS

    load_x = pltpu.make_async_copy(x_hbm, x_ref, in_x.at[0])
    bounds = (*GROUPS, distinct)

    def load_gates(i):
        some = pl.ds(bounds[i], bounds[i + 1] - bounds[i])
        return pltpu.make_async_copy(g_hbm.at[:, some], g_ref.at[:, some], in_g.at[i])

    load_gates(0).start()
    load_x.start()
    for i in range(1, len(GROUPS)):
        load_gates(i).start()
    me = lax.axis_index("node")
    barrier = pltpu.get_barrier_semaphore()
    for i in range(1, nodes):
        pl.semaphore_signal(barrier, inc=1, device_id={"node": me ^ i}, device_id_type=pl.DeviceIdType.MESH)

    ready = set()
    loaded = set()

    def arrive(m):
        i = sum(m >= bound for bound in GROUPS) - 1
        if i not in loaded:
            loaded.add(i)
            load_gates(i).wait()

    def gate(g):
        m = g % distinct
        if m not in ready:
            ready.add(m)
            arrive(m)
            prepare(g_ref, gc, m, g % 4 == 1)
        return gc[m]

    def store(ref, first, y):
        ref[0, pl.ds(first, y.shape[0]), :] = y[:, :LANES]
        ref[1, pl.ds(first, y.shape[0]), :] = y[:, LANES:]

    def load_quarters(ref, firsts):
        return jnp.concatenate(
            [
                jnp.concatenate([ref[0, pl.ds(first, quarter), :], ref[1, pl.ds(first, quarter), :]], 0)
                for first in firsts
            ],
            1,
        )

    def store_quarters(ref, firsts, y):
        for i, first in enumerate(firsts):
            ref[0, pl.ds(first, quarter), :] = y[:ORDER, i * LANES : (i + 1) * LANES]
            ref[1, pl.ds(first, quarter), :] = y[ORDER:, i * LANES : (i + 1) * LANES]

    def strided(g, src, dst):
        matrix = gate(g)
        for pair in range(2):
            x = jnp.concatenate(
                [
                    jnp.concatenate([src[part, pl.ds(2 * pair + c, ORDER, stride=4), :] for part in range(2)], 0)
                    for c in range(2)
                ],
                1,
            )
            y = left(matrix, x)
            for c in range(2):
                for part in range(2):
                    dst[part, pl.ds(2 * pair + c, ORDER, stride=4), :] = y[
                        part * ORDER : (part + 1) * ORDER, c * LANES : (c + 1) * LANES
                    ]

    def finish(ref, some, sem):
        pltpu.make_async_copy(ref.at[:, pl.ds(0, some), :], ref.at[:, pl.ds(0, some), :], sem).wait()

    def halves_of(g, k):
        arrive(g % distinct)
        prepare_halves(g_ref, gh, k, g % distinct)

    def strided_half(k, src, dst, h, add):
        matrix = gh[k, h]
        base = pl.multiple_of(h * (rows // 2), rows // 2)
        for pair in range(2):
            x = jnp.concatenate(
                [
                    jnp.concatenate(
                        [src[part, pl.ds(base + 2 * pair + c, ORDER // 2, stride=4), :] for part in range(2)], 0
                    )
                    for c in range(2)
                ],
                1,
            )
            y = left(matrix, x)
            for c in range(2):
                for part in range(2):
                    z = y[part * ORDER : (part + 1) * ORDER, c * LANES : (c + 1) * LANES]
                    some = pl.ds(2 * pair + c, ORDER, stride=4)
                    if add:
                        z = z + dst[part, some, :]
                    dst[part, some, :] = z

    def middle(g, y):
        return swap_blocks(left(gate(g), swap_blocks(y)))

    def low_gates(x):
        y = to_right(middle(5, to_left(right(gate(4), x))))
        return right(gate(8), y)

    halves = [(0, quarter, 2 * quarter, 3 * quarter)]
    gate(0)
    gate(1)
    load_x.wait()
    x = jnp.concatenate([x_ref[pl.ds(part, rows, stride=2), :] for part in range(2)], 1)
    store(sa, 0, to_right(middle(1, to_left(right(gate(0), x)))))
    gate(2)
    gate(3)
    strided(2, sa, sb)

    slot = reversed3(me & 7)
    part1 = rows // 8
    for orders in ((1,), (0,), (3, 2)):
        spots = [(slot >> 1) ^ order for order in orders]
        firsts = [pl.multiple_of(a * quarter, quarter) for a in spots]
        y = left(gate(3), load_quarters(sb, firsts))
        if max(orders) < 2:
            store_quarters(sc, firsts, y)
        else:
            y = low_gates(to_right(y))
            for i, first in enumerate(firsts):
                store(sc, first, y[i * quarter : (i + 1) * quarter])
        if 1 in orders:
            pl.semaphore_wait(barrier, nodes - 1)
        for order, a, low in [(order, a, low) for order, a in zip(orders, spots) for low in (1, 0)]:
            if order == 0 and low == 0:
                mine = pl.ds(pl.multiple_of(slot * part1, part1), part1)
                r1[:, mine, :] = sc[:, mine, :]
                continue
            block = 2 * a + ((slot & 1) ^ low)
            index = 2 * order + low
            pltpu.make_async_remote_copy(
                src_ref=sc.at[:, pl.ds(pl.multiple_of(block * part1, part1), part1), :],
                dst_ref=r1.at[:, pl.ds(pl.multiple_of(slot * part1, part1), part1), :],
                send_sem=send1.at[0],
                recv_sem=recv1.at[index // 4],
                device_id={"node": (me & ~7) | reversed3(block)},
                device_id_type=pl.DeviceIdType.MESH,
            ).start()

    halves_of(6, 0)
    gate(7)
    gate(9)

    finish(r1, 3 * part1, recv1.at[0])
    firsts = [pl.multiple_of((slot ^ index) * part1, part1) for index in range(4)]
    x = jnp.concatenate(
        [jnp.concatenate([r1[part, pl.ds(first, part1), :] for part in range(2)], 1) for first in firsts], 0
    )
    y = low_gates(x)
    for i, first in enumerate(firsts):
        store(sa, first, y[i * part1 : (i + 1) * part1])
    strided_half(0, sa, sb, slot >> 2, False)
    finish(r1, 4 * part1, recv1.at[1])
    strided_half(0, r1, sb, (slot >> 2) ^ 1, True)

    part2 = rows // nodes
    per = nodes // QUARTERS
    early = part2 * LANES >= 1 << 11
    mine = pl.ds(pl.multiple_of(me * part2, part2), part2)
    spot = me // per
    even = 1 - (spot & 1)
    side = me // (nodes // 2)

    def second(index, far):
        block = me ^ index
        return pltpu.make_async_remote_copy(
            src_ref=sd.at[:, pl.ds(pl.multiple_of(block * part2, part2), part2), :],
            dst_ref=r2.at[:, mine, :],
            send_sem=send2.at[0],
            recv_sem=recv2.at[far],
            device_id={"node": block},
            device_id_type=pl.DeviceIdType.MESH,
        )

    for phase, orders in enumerate(((3 - even,), (1, 2 + even), (0,))):
        firsts = [pl.multiple_of((spot ^ order) * quarter, quarter) for order in orders]
        y = left(gate(7), load_quarters(sb, firsts))
        if early and phase > 0:
            y = middle(9, y)
        store_quarters(sd, firsts, y)
        for order, low in [(order, low) for order in orders for low in range(per - 1, -1, -1)]:
            if isinstance(order, int) and order == 0 and low == 0:
                r2[:, mine, :] = sd[:, mine, :]
            else:
                second(order * per + low, 0 if isinstance(order, int) and order < 2 else 1).start()

    halves_of(10, 1)
    gate(11)
    finish(sc, 7 * part1, send1.at[0])

    def arrive_half(far):
        finish(r2, (nodes // 2 - 1 + far) * part2, recv2.at[far])

    if early:

        @pl.when(even == 0)
        def _():
            arrive_half(0)

        @pl.when(even == 1)
        def _():
            arrive_half(1)
            firsts = [pl.multiple_of((spot ^ order) * quarter, quarter) for order in (2, 3)]
            store_quarters(r2, firsts, middle(9, load_quarters(r2, firsts)))

        strided_half(1, r2, sa, side ^ even, False)

        @pl.when(even == 0)
        def _():
            arrive_half(1)

        @pl.when(even == 1)
        def _():
            arrive_half(0)

        strided_half(1, r2, sa, side ^ (1 - even), True)
    else:
        arrive_half(0)
        arrive_half(1)
        for firsts in halves:
            store_quarters(sb, firsts, middle(9, load_quarters(r2, firsts)))
        for far in range(2):
            strided_half(1, sb, sa, side ^ far, far == 1)
    for firsts in halves:
        y = left(gate(11), load_quarters(sa, firsts))
        for i, first in enumerate(firsts):
            for part in range(2):
                o_ref[pl.ds(2 * first + part, quarter, stride=2), :] = y[
                    part * ORDER : (part + 1) * ORDER, i * LANES : (i + 1) * LANES
                ]
    finish(sd, (nodes - 1) * part2, send2.at[0])


def body(nodes, amplitudes, gates):
    total = amplitudes.shape[1]
    distinct = gates.shape[1]
    rows = total // LANES
    x = amplitudes.reshape(2, rows, LANES).transpose(1, 0, 2).reshape(2 * rows, LANES)
    state = pltpu.VMEM((2, rows, LANES), F32)
    out = pl.pallas_call(
        functools.partial(kernel, nodes, distinct),
        out_shape=jax.ShapeDtypeStruct((2 * rows, LANES), F32),
        in_specs=[pl.BlockSpec(memory_space=pltpu.HBM)] * 2,
        out_specs=pl.BlockSpec(memory_space=pltpu.VMEM),
        scratch_shapes=[
            pltpu.VMEM((2 * rows, LANES), F32),
            pltpu.VMEM(gates.shape, F32),
            pltpu.VMEM((distinct, 2 * ORDER, 6 * ORDER), BF16),
            pltpu.VMEM((2, 2, 2 * ORDER, 3 * ORDER), BF16),
            state,
            state,
            state,
            state,
            state,
            state,
            pltpu.SemaphoreType.DMA((1,)),
            pltpu.SemaphoreType.DMA((len(GROUPS),)),
            pltpu.SemaphoreType.DMA((1,)),
            pltpu.SemaphoreType.DMA((2,)),
            pltpu.SemaphoreType.DMA((1,)),
            pltpu.SemaphoreType.DMA((2,)),
        ],
        compiler_params=pltpu.CompilerParams(collective_id=0, has_side_effects=True, vmem_limit_bytes=53 << 20),
        name="circuit",
    )(x, gates)
    return out.reshape(rows, 2, LANES).transpose(1, 0, 2).reshape(2, total)


def solution(mesh):
    spec = P(None, ("paths", "node"))
    return jax.shard_map(
        functools.partial(body, mesh.shape["node"]), mesh=mesh, in_specs=(spec, P()), out_specs=spec, check_vma=False
    )
```
